32 devices in a mesh: groups: 2 (over x), wide: 8 (over z, y), narrow: 2 (over core).
Axes of the slice: x: 2, y: 2, z: 4, core: 2. Of those that a mesh axis runs over, the one named last changes fastest.
Arguments:
- tokens: bfloat16 [2048, 2048], P(('groups', 'wide', 'narrow')), parts along dimension 0, may hold values from -6 to 6
- gate_wts: bfloat16 [2048, 8], P(('groups', 'wide', 'narrow')), parts along dimension 0, may hold values from 0.099609375 to 1
- expert_ids: int32 [2048, 8], P(('groups', 'wide', 'narrow')), parts along dimension 0, may hold values from 0 to 23, as said below
- replica: int32 [2048, 8], P(('groups', 'wide', 'narrow')), parts along dimension 0, may hold values from 0 to 1, as said below
- w_gate: bfloat16 [32, 2048, 384], P(('wide', 'narrow')), may hold values from -0.125 to 0.125
- w_up: bfloat16 [32, 2048, 384], P(('wide', 'narrow')), may hold values from -0.125 to 0.125
- w_down: bfloat16 [32, 384, 2048], P(('wide', 'narrow')), may hold values from -0.3125 to 0.3125
- queries: bfloat16 [64, 32, 128], P(('groups', 'wide', 'narrow')), parts along dimension 0, may hold values from -80 to 80
- k_cache: bfloat16 [64, 640, 4, 128], P(('groups', 'wide', 'narrow')), parts along dimension 0, may hold values from -4 to 4
- value_cache: bfloat16 [64, 640, 4, 128], P(('groups', 'wide', 'narrow')), parts along dimension 0, may hold values from -5 to 5
- lengths: int32 [64], P(('groups', 'wide', 'narrow')), parts along dimension 0, may hold values from 80 to 640, as said below
Outputs:
- routed_out: bfloat16 [2048, 2048], P(('groups', 'wide', 'narrow')), parts along dimension 0
- attn_out: bfloat16 [64, 4096], P(('groups', 'wide', 'narrow')), parts along dimension 0
The draws below stay inside these ranges and needn't reach their ends.
There are 2 independent parts, one for each index of `groups`. The reference program is written for one: setup_inputs(seed, part) draws one part's arguments, and reference() takes and returns one part's arrays. A program takes and returns all parts, laid end to end along the dimension named above; an argument that names none is the same for every part. Nothing has to cross between parts.
Inputs may be any that keep to these rules, and one draw needn't show every extreme that they name: `expert_ids`: each row names 8 different experts. Counted over the rows of one device (aligned blocks of 64 rows), the rows whose slots lie on one device number at most 64; one device, the same for every block of a draw, gets exactly 64 rows from every block. `replica`: 1 only where the named expert is below 8. `lengths`: one request of each draw has exactly 640 live positions.
All inputs are finite; a program needn't handle non-finite values.
Results may differ from the reference program's by a relative error of at most 0.008.
Values may be sent and summed in bfloat16 or wider, within the bound.
A program may use at most 128 MiB of HBM per device.

```python
import math
import jax
import jax.numpy as jnp
from jax import lax

D = 2048
HE = 384
TOPK = 8
SLOT_DEV = 2
QUERY_HEADS = 32
KEY_VALUE_HEADS = 4
HEAD_SIZE = 128
CACHE_POSITIONS = 640
ROWS = 64
DEVS_PART = 16
EXPERTS = 24
REPLICAS = 8
SLOTS = 32
CAP = 64
TOKENS = 1024
REQUEST_COUNT = 32


def route_slots(key):
    key = jax.random.fold_in(key, 11)
    first, second = jax.random.split(key, 2)
    quarter = DEVS_PART // 4
    upper = 3 * DEVS_PART // 4
    pairs_total = ROWS * TOPK
    remaining = pairs_total - 2 * CAP
    even_share = remaining // (DEVS_PART - 1)
    spare_cut = remaining % (DEVS_PART - 1)
    hottest = quarter + jax.random.randint(first, (), 0, DEVS_PART // 2)
    devices = jnp.arange(DEVS_PART, dtype=jnp.int32)
    unit_of = jnp.where(devices >= upper, devices - upper, devices).astype(jnp.int32)
    is_upper = (devices >= upper).astype(jnp.int32)
    position = jnp.arange(DEVS_PART, dtype=jnp.int32)
    counts = jnp.where(position == 0, 2 * CAP, even_share + (position - 1 < spare_cut).astype(jnp.int32)).astype(jnp.int32)
    bounds = jnp.cumsum(counts)
    pairs = jnp.arange(pairs_total, dtype=jnp.int32)
    place = jnp.sum((bounds[None, :] <= pairs[:, None]).astype(jnp.int32), axis=1).astype(jnp.int32)
    within = pairs % (2 * ROWS)
    row_of = within // 2
    col_of = 2 * (pairs // (2 * ROWS)) + pairs % 2
    bit_of = pairs % 2

    def block(block_key):
        key_first_split, key_second_split = jax.random.split(block_key, 2)
        ranking = jax.random.permutation(key_first_split, upper).astype(jnp.int32)[unit_of]
        score = jnp.where(devices == hottest, -1, 2 * ranking + is_upper).astype(jnp.int32)
        sequence = jnp.argsort(score, stable=True).astype(jnp.int32)
        dev_of = sequence[place]
        slots_blk = jnp.zeros((ROWS, TOPK), jnp.int32).at[row_of, col_of].set(SLOT_DEV * dev_of + bit_of)
        shuffle = jax.random.permutation(key_second_split, ROWS)
        return slots_blk[shuffle]
    keys = jax.random.split(second, DEVS_PART)
    return lax.map(block, keys).reshape(TOKENS, TOPK).astype(jnp.int32)


def draw_expert_ids(key, part):
    slots_all = route_slots(key)
    return jnp.where(slots_all >= EXPERTS, slots_all - EXPERTS, slots_all).astype(jnp.int32)


def draw_replica(key, part):
    slots_all = route_slots(key)
    return (slots_all >= EXPERTS).astype(jnp.int32)


def draw_lengths(key, part):
    key = jax.random.fold_in(key, 5)
    key_first_split, key_second_split = jax.random.split(key, 2)
    value_rows = jax.random.randint(key_first_split, (REQUEST_COUNT,), CACHE_POSITIONS // 8, CACHE_POSITIONS + 1)
    where_full = jax.random.randint(key_second_split, (), 0, REQUEST_COUNT)
    return value_rows.at[where_full].set(CACHE_POSITIONS).astype(jnp.int32)


def draw_k_cache(key, part):
    inner_product = jax.random.fold_in(key, 1)
    value_rows = jnp.clip(jax.random.normal(inner_product, (REQUEST_COUNT, CACHE_POSITIONS, KEY_VALUE_HEADS, HEAD_SIZE), jnp.float32), -4.0, 4.0)
    return value_rows.astype(jnp.bfloat16)


def draw_queries(key, part):
    inner_product = jax.random.fold_in(key, 2)
    value_rows = jnp.clip(jax.random.normal(inner_product, (REQUEST_COUNT, QUERY_HEADS, HEAD_SIZE), jnp.float32), -4.0, 4.0)
    return value_rows.astype(jnp.bfloat16)


def level_of(own_key, extent, pieces, smallest, top_value):
    loudness, own = 1.0, jax.random.fold_in(own_key, 6)
    for dim, parts in pieces:
        steps = jnp.exp(jax.random.uniform(jax.random.fold_in(own, dim), (parts,), jnp.float32, smallest / len(pieces), top_value / len(pieces)))
        loudness = loudness * jnp.repeat(steps, extent[dim] // parts).reshape([-1 if axis == dim else 1 for axis in range(len(extent))])
    return loudness


def centred(own_key, extent, width, reach, cuts=(), kind=jnp.bfloat16):
    gain = level_of(own_key, extent, cuts, -0.22, 0.18) if cuts else 1.0
    values = jax.random.normal(own_key, extent, jnp.float32) * width * gain
    return jnp.minimum(jnp.maximum(values, -reach), reach).astype(kind)


def setup_inputs(seed: int = 0, part: int = 0) -> dict:
    arg_keys = jax.random.split(jax.random.key(seed), 12)
    part_splits = jax.random.split(jax.random.fold_in(arg_keys[11], part), 12)
    return {
        "tokens": centred(part_splits[0], (TOKENS, D), 1.0, 6.0, ((0, 16),)),
        "gate_wts": jnp.clip(jnp.exp(math.log(1.0) - 2.306499 * jax.random.uniform(part_splits[1], (TOKENS, TOPK), jnp.float32) ** level_of(part_splits[1], (TOKENS, TOPK), ((0, 16),), -0.2, 0.2)), 0.099609375, 1.0).astype(jnp.bfloat16),
        "expert_ids": draw_expert_ids(jax.random.fold_in(jax.random.fold_in(arg_keys[11], part), 71), part),
        "replica": draw_replica(jax.random.fold_in(jax.random.fold_in(arg_keys[11], part), 71), part),
        "w_gate": centred(arg_keys[4], (SLOTS, D, HE), D ** -0.5, 0.125, ((0, 16),)),
        "w_up": centred(arg_keys[5], (SLOTS, D, HE), D ** -0.5, 0.125, ((0, 16),)),
        "w_down": centred(arg_keys[6], (SLOTS, HE, D), HE ** -0.5, 0.3125, ((0, 16),)),
        "queries": draw_queries(jax.random.fold_in(jax.random.fold_in(arg_keys[11], part), 71), part),
        "k_cache": draw_k_cache(jax.random.fold_in(jax.random.fold_in(arg_keys[11], part), 71), part),
        "value_cache": centred(part_splits[9], (REQUEST_COUNT, CACHE_POSITIONS, KEY_VALUE_HEADS, HEAD_SIZE), 1.0, 5.0, ((0, 16),)),
        "lengths": draw_lengths(jax.random.fold_in(jax.random.fold_in(arg_keys[11], part), 71), part),
    }


def attend(queries, k_cache, value_cache, lengths):
    reqs, heads, head_dim = queries.shape
    kv_heads = k_cache.shape[2]
    group = heads // kv_heads
    grouped = queries.reshape(reqs, kv_heads, group, head_dim).astype(jnp.float32)
    scores = jnp.einsum("rkgd,rlkd->rkgl", grouped, k_cache.astype(jnp.float32)) * (head_dim ** -0.5)
    valid = jnp.arange(k_cache.shape[1], dtype=jnp.int32)[None, :] < lengths[:, None]
    valid = valid[:, None, None, :]
    scores = jnp.where(valid, scores, -1e30)
    top = jnp.max(scores, axis=-1, keepdims=True)
    expd = jnp.where(valid, jnp.exp(scores - top), 0.0)
    probs = (expd / jnp.sum(expd, axis=-1, keepdims=True)).astype(jnp.bfloat16)
    mixed = jnp.einsum("rkgl,rlkd->rkgd", probs.astype(jnp.float32), value_cache.astype(jnp.float32))
    return mixed.astype(jnp.bfloat16).reshape(reqs, heads * head_dim)


def reference(tokens, gate_wts, expert_ids, replica, w_gate, w_up, w_down, queries, k_cache, value_cache, lengths):
    phys_slot = jnp.where((replica == 1) & (expert_ids < REPLICAS), expert_ids + EXPERTS, expert_ids).astype(jnp.int32)
    owner_dev = phys_slot // SLOT_DEV
    slot_bit = phys_slot % SLOT_DEV
    gate_values = gate_wts.astype(jnp.float32)
    bound = DEVS_PART * CAP

    def per_device(total, device):
        hits_mask = owner_dev == device
        routed_to = jnp.any(hits_mask, axis=1)
        order = jnp.argsort(jnp.where(routed_to, 0, 1).astype(jnp.int32), stable=True)[:bound].astype(jnp.int32)
        chosen = tokens[order]
        result = jnp.zeros((bound, D), jnp.float32)
        for j in range(SLOT_DEV):
            coefficients = jnp.sum(jnp.where(hits_mask & (slot_bit == j), gate_values, 0.0), axis=1)[order]
            index = device * SLOT_DEV + j
            gated = jnp.dot(chosen, w_gate[index], preferred_element_type=jnp.float32)
            upward = jnp.dot(chosen, w_up[index], preferred_element_type=jnp.float32)
            hidden = (jax.nn.silu(gated) * upward).astype(jnp.bfloat16)
            result = result + coefficients[:, None] * jnp.dot(hidden, w_down[index], preferred_element_type=jnp.float32)
        rounded = lax.optimization_barrier(result.astype(jnp.bfloat16)).astype(jnp.float32)
        return total.at[order].add(rounded), None

    total, _ = lax.scan(per_device, jnp.zeros((TOKENS, D), jnp.float32), jnp.arange(DEVS_PART, dtype=jnp.int32))
    routed_out = total.astype(jnp.bfloat16)
    return routed_out, attend(queries, k_cache, value_cache, lengths)
```

```python
import functools
import jax
import jax.numpy as jnp
from jax import lax
from jax.experimental import pallas as pl
from jax.experimental.pallas import tpu as pltpu
from jax.sharding import PartitionSpec as P

SLOT_DEV = 2
LANES = 128
MESH = pl.DeviceIdType.MESH


def attend(queries, k_cache, value_cache, lengths):
    reqs, heads, head_dim = queries.shape
    kv_heads = k_cache.shape[2]
    group = heads // kv_heads
    grouped = queries.reshape(reqs, kv_heads, group, head_dim)
    scores = jnp.einsum(
        "rkgd,rlkd->rkgl", grouped, k_cache, preferred_element_type=jnp.float32
    ) * head_dim ** (-0.5)
    valid = jnp.arange(k_cache.shape[1], dtype=jnp.int32)[None, :] < lengths[:, None]
    valid = valid[:, None, None, :]
    scores = jnp.where(valid, scores, -1e30)
    top = jnp.max(scores, axis=-1, keepdims=True)
    expd = jnp.where(valid, jnp.exp(scores - top), 0.0)
    probs = (expd / jnp.sum(expd, axis=-1, keepdims=True)).astype(jnp.bfloat16)
    mixed = jnp.einsum("rkgl,rlkd->rkgd", probs, value_cache, preferred_element_type=jnp.float32)
    return mixed.astype(jnp.bfloat16).reshape(reqs, heads * head_dim)


def exchange_local(
    tokens,
    gate_wts,
    expert_ids,
    replica,
    w_gate,
    w_up,
    w_down,
    queries,
    k_cache,
    value_cache,
    lengths,
):
    wide_count = lax.axis_size("wide")
    narrow_count = lax.axis_size("narrow")
    devices = wide_count * narrow_count
    experts = 3 * devices // 2
    spares = devices // 2
    rows_here = tokens.shape[0]
    model_width = tokens.shape[1]
    top_count = expert_ids.shape[1]
    capacity = min(rows_here, 2 * rows_here * top_count // devices)
    phys_slot = jnp.where((replica == 1) & (expert_ids < spares), expert_ids + experts, expert_ids)
    owner_dev = phys_slot // SLOT_DEV
    slot_bit = phys_slot % SLOT_DEV
    owners = jnp.arange(devices, dtype=jnp.int32)
    hits_mask = owner_dev[:, :, None] == owners[None, None, :]
    routed_to = jnp.any(hits_mask, axis=1).astype(jnp.float32)
    gate_values = gate_wts.astype(jnp.float32)
    coefficients = jnp.stack(
        [
            jnp.sum(
                jnp.where(hits_mask & (slot_bit[:, :, None] == j), gate_values[:, :, None], 0.0),
                axis=1,
            )
            for j in range(SLOT_DEV)
        ],
        axis=-1,
    )
    row_ids = jnp.arange(rows_here, dtype=jnp.int32)
    earlier = (row_ids[None, :] < row_ids[:, None]).astype(jnp.float32)
    before = jnp.dot(earlier, routed_to, precision=lax.Precision.HIGHEST)
    positions = jnp.arange(capacity, dtype=jnp.float32)
    slots_map = (routed_to[:, :, None] * (before[:, :, None] == positions[None, None, :])).astype(
        jnp.bfloat16
    )
    outgoing = jnp.einsum(
        "rdc,rm->dcm", slots_map, tokens, preferred_element_type=jnp.float32
    ).astype(jnp.bfloat16)
    weights_out = jnp.einsum(
        "rdc,rdj->dcj",
        slots_map,
        coefficients.astype(jnp.bfloat16),
        preferred_element_type=jnp.float32,
    ).astype(jnp.bfloat16)
    arrived = lax.all_to_all(outgoing, ("wide", "narrow"), split_axis=0, concat_axis=0, tiled=True)
    shares = lax.all_to_all(
        weights_out, ("wide", "narrow"), split_axis=0, concat_axis=0, tiled=True
    )
    flat = arrived.reshape(-1, model_width)
    share_flat = shares.reshape(-1, SLOT_DEV).astype(jnp.float32)
    result = jnp.zeros(flat.shape, jnp.float32)
    for j in range(SLOT_DEV):
        gated = jnp.dot(flat, w_gate[j], preferred_element_type=jnp.float32)
        upward = jnp.dot(flat, w_up[j], preferred_element_type=jnp.float32)
        hidden = (jax.nn.silu(gated) * upward).astype(jnp.bfloat16)
        result = result + share_flat[:, j : j + 1] * jnp.dot(
            hidden, w_down[j], preferred_element_type=jnp.float32
        )
    returned = lax.all_to_all(
        result.astype(jnp.bfloat16).reshape(arrived.shape),
        ("wide", "narrow"),
        split_axis=0,
        concat_axis=0,
        tiled=True,
    )
    attn_out = attend(queries, k_cache, value_cache, lengths)
    routed_out = jnp.einsum(
        "rdc,dcm->rm", slots_map, returned, preferred_element_type=jnp.float32
    ).astype(jnp.bfloat16)
    return (routed_out, attn_out)


def ring_place(wide, count):
    odd = wide % 2
    return (1 - odd) * (wide // 2) + odd * (count - 1 - wide // 2)


def ring_wide(place, count):
    upper = place // (count // 2)
    return (1 - upper) * (2 * place) + upper * (2 * (count - 1 - place) + 1)


def kernel(
    count,
    kv_heads,
    x_ref,
    coef_ref,
    gate_hbm,
    up_hbm,
    down_hbm,
    q_ref,
    k_hbm,
    v_hbm,
    len_ref,
    out_ref,
    attn_ref,
    xa,
    po,
    sb,
    rb,
    tb,
    w_in,
    w_out,
    k_buf,
    v_buf,
    w_sem,
    kv_sem,
    ag_send,
    ag_recv,
    sib_send,
    sib_recv,
    own_send,
    own_recv,
    part_send,
    part_recv,
    part0_send,
    part0_recv,
    rs_send,
    rs_recv,
):
    rows, width = x_ref.shape
    half = rows // 2
    hid = gate_hbm.shape[2]
    arrivals = count - 1
    wide = lax.axis_index("wide")
    core = lax.axis_index("narrow")
    other = 1 - core
    place = ring_place(wide, count)
    after = ring_wide((place + 1) % count, count)
    before = ring_wide((place + count - 1) % count, count)
    me = wide * 2 + core
    targets = ({"wide": after}, {"wide": before})
    sibling = {"narrow": other}

    def aligned(index, size):
        return pl.ds(pl.multiple_of(index * size, size), size)

    def remote(src, dst, send, recv, device):
        return pltpu.make_async_remote_copy(
            src_ref=src, dst_ref=dst, send_sem=send, recv_sem=recv, device_id=device, device_id_type=MESH
        )

    kv_copies = [
        pltpu.make_async_copy(k_hbm, k_buf, kv_sem.at[0]),
        pltpu.make_async_copy(v_hbm, v_buf, kv_sem.at[1]),
    ]
    w_copies = []
    for j in range(SLOT_DEV):
        w_copies += [
            pltpu.make_async_copy(
                gate_hbm.at[j], w_in.at[:, pl.ds(2 * j * hid, hid)], w_sem.at[3 * j]
            ),
            pltpu.make_async_copy(
                up_hbm.at[j], w_in.at[:, pl.ds((2 * j + 1) * hid, hid)], w_sem.at[3 * j + 1]
            ),
            pltpu.make_async_copy(
                down_hbm.at[j], w_out.at[pl.ds(j * hid, hid)], w_sem.at[3 * j + 2]
            ),
        ]
    for copy in kv_copies + w_copies:
        copy.start()
    xa[0, aligned(core, rows), :width] = x_ref[...]
    xa[0, aligned(core, rows), width:] = coef_ref[...]

    barrier = pltpu.get_barrier_semaphore()
    for device in (*targets, sibling):
        pl.semaphore_signal(barrier, inc=1, device_id=device, device_id_type=MESH)
    pl.semaphore_wait(barrier, 3)

    def unit(i, way):
        return i + 1, aligned(way * 2 + core, half)

    def gather_own(i, way):
        piece, at = unit(i, way)
        part = i if way == 0 else 1 - i
        return remote(
            xa.at[0, aligned(core * 2 + part, half)],
            xa.at[piece, at],
            ag_send.at[way, i],
            ag_recv.at[way, i],
            targets[way],
        )

    def gather_on(i, way):
        piece, at = unit(i, way)
        return remote(
            xa.at[piece - 2, at], xa.at[piece, at], ag_send.at[way, i], ag_recv.at[way, i], targets[way]
        )

    def landed(i, way):
        piece, at = unit(i, way)
        return remote(
            xa.at[piece, at], xa.at[piece, at], ag_send.at[way, i], ag_recv.at[way, i], targets[way]
        )

    def share(i, way):
        piece, at = unit(i, way)
        return remote(xa.at[piece, at], xa.at[piece, at], sib_send.at[way, i], sib_recv.at[way, i], sibling)

    def share_own():
        at = aligned(core, rows)
        return remote(xa.at[0, at], xa.at[0, at], own_send, own_recv, sibling)

    def give(i, way):
        return remote(
            po.at[i + 1, aligned(way * 2 + other, half)],
            sb.at[i + 1, pl.ds(way * half, half)],
            part_send.at[way, i],
            part_recv.at[way, i],
            sibling,
        )

    def give_own():
        return remote(po.at[0, aligned(other, rows)], sb.at[0], part0_send, part0_recv, sibling)

    def collect(r, way):
        return remote(tb.at[way, r], rb.at[way, r], rs_send.at[way, r], rs_recv.at[way, r], targets[1 - way])

    for i in range(2):
        for way in range(2):
            gather_own(i, way).start()
    share_own().start()

    for copy in kv_copies:
        copy.wait()
    heads, head_dim = q_ref.shape[1:]
    group = heads // kv_heads
    shape = (heads, k_buf.shape[1])
    col = lax.broadcasted_iota(jnp.int32, shape, 1)
    row = lax.broadcasted_iota(jnp.int32, shape, 0)
    kind = jnp.zeros(shape, jnp.int32)
    for g in range(1, kv_heads):
        kind = kind + (row >= g * group).astype(jnp.int32)
    mine = jnp.bitwise_and(col, kv_heads - 1) == kind
    for r in range(q_ref.shape[0]):
        scores = lax.dot_general(
            q_ref[r], k_buf[r], (((1,), (1,)), ((), ())), preferred_element_type=jnp.float32
        ) * head_dim ** (-0.5)
        valid = mine & (col < len_ref[r] * kv_heads)
        scores = jnp.where(valid, scores, -1e30)
        top = jnp.max(scores, axis=-1, keepdims=True)
        expd = jnp.where(valid, jnp.exp(scores - top), 0.0)
        probs = (expd / jnp.sum(expd, axis=-1, keepdims=True)).astype(jnp.bfloat16)
        mixed = jnp.dot(probs, v_buf[r], preferred_element_type=jnp.float32)
        attn_ref[r] = mixed.astype(jnp.bfloat16)

    for copy in w_copies:
        copy.wait()

    def experts(t):
        x = xa[t, :, :width]
        shares = xa[t, :, width:].astype(jnp.float32)
        lane = lax.broadcasted_iota(jnp.int32, shares.shape, 1)
        hidden = []
        for j in range(SLOT_DEV):
            both = jnp.dot(
                x, w_in[:, 2 * j * hid : 2 * (j + 1) * hid], preferred_element_type=jnp.float32
            )
            gated, upward = both[:, :hid], both[:, hid:]
            weight = jnp.sum(
                jnp.where(lane == me * SLOT_DEV + j, shares, 0.0), axis=1, keepdims=True
            )
            hidden.append((weight * (gated / (1.0 + jnp.exp(-gated)) * upward)).astype(jnp.bfloat16))
        hidden = jnp.concatenate(hidden, axis=1)
        po[t] = jnp.dot(hidden, w_out[...], preferred_element_type=jnp.float32).astype(jnp.bfloat16)

    def step(t, _):
        @pl.when(t < arrivals)
        def _():
            for way in range(2):
                landed(t, way).wait_recv()

            @pl.when(t + 2 < arrivals)
            def _():
                for way in range(2):
                    gather_on(t + 2, way).start()

            for way in range(2):
                share(t, way).start()

        @pl.when(t == 0)
        def _():
            share_own().wait_recv()

        @pl.when(t > 0)
        def _():
            for way in range(2):
                share(t - 1, way).wait_recv()

        experts(t)

        @pl.when(t == 0)
        def _():
            give_own().start()

        @pl.when(t > 0)
        def _():
            for way in range(2):
                give(t - 1, way).start()

        return _

    lax.fori_loop(0, count, step, None)

    def back(r, first):
        i = arrivals - 1 - r
        for way in range(2):
            give(i, way).wait_recv()
            piece, at = unit(i, way)
            total = po[piece, at].astype(jnp.float32) + sb[piece, way * half : (way + 1) * half].astype(
                jnp.float32
            )
            if not first:
                collect(r - 2, way).wait_recv()
                total = total + rb[way, r - 2].astype(jnp.float32)
            tb[way, r] = total.astype(jnp.bfloat16)
            collect(r, way).start()

    for r in range(2):
        back(r, True)

    def back_on(r, _):
        back(r, False)
        return _

    lax.fori_loop(2, arrivals, back_on, None)

    give_own().wait_recv()
    for way in range(2):
        collect(arrivals - 2, way).wait_recv()
        collect(arrivals - 1, way).wait_recv()
    for part in range(2):
        total = po[0, aligned(core * 2 + part, half)].astype(jnp.float32) + sb[
            0, part * half : (part + 1) * half
        ].astype(jnp.float32)
        for way in range(2):
            i = part if way == 0 else 1 - part
            total = total + rb[way, arrivals - 1 - i].astype(jnp.float32)
        out_ref[part * half : (part + 1) * half] = total.astype(jnp.bfloat16)

    share_own().wait_send()
    give_own().wait_send()

    def drain(i, _):
        for way in range(2):
            landed(i, way).wait_send()
            share(i, way).wait_send()
            give(i, way).wait_send()
            collect(i, way).wait_send()
        return _

    lax.fori_loop(0, arrivals, drain, None)


def fused(tokens, coefs, w_gate, w_up, w_down, queries, k_cache, value_cache, lengths, budget):
    count = lax.axis_size("wide")
    rows, width = tokens.shape
    half = rows // 2
    lanes = coefs.shape[1]
    hid = w_gate.shape[2]
    reqs, positions, kv_heads, head_dim = k_cache.shape
    bf16, dma = jnp.bfloat16, pltpu.SemaphoreType.DMA
    vmem, hbm = pl.BlockSpec(memory_space=pltpu.VMEM), pl.BlockSpec(memory_space=pl.ANY)
    arrivals = count - 1
    pairs = dma((2, arrivals))
    routed, attn = pl.pallas_call(
        functools.partial(kernel, count, kv_heads),
        out_shape=(
            jax.ShapeDtypeStruct(tokens.shape, bf16),
            jax.ShapeDtypeStruct(queries.shape, bf16),
        ),
        in_specs=[vmem, vmem, hbm, hbm, hbm, vmem, hbm, hbm, pl.BlockSpec(memory_space=pltpu.SMEM)],
        out_specs=(vmem, vmem),
        scratch_shapes=[
            pltpu.VMEM((count, 2 * rows, width + lanes), bf16),
            pltpu.VMEM((count, 2 * rows, width), bf16),
            pltpu.VMEM((count, rows, width), bf16),
            pltpu.VMEM((2, arrivals, half, width), bf16),
            pltpu.VMEM((2, arrivals, half, width), bf16),
            pltpu.VMEM((width, 2 * SLOT_DEV * hid), bf16),
            pltpu.VMEM((SLOT_DEV * hid, width), bf16),
            pltpu.VMEM((reqs, positions * kv_heads, head_dim), bf16),
            pltpu.VMEM((reqs, positions * kv_heads, head_dim), bf16),
            dma((3 * SLOT_DEV,)),
            dma((2,)),
            pairs,
            pairs,
            pairs,
            pairs,
            dma(()),
            dma(()),
            pairs,
            pairs,
            dma(()),
            dma(()),
            pairs,
            pairs,
        ],
        compiler_params=pltpu.CompilerParams(
            collective_id=0, has_side_effects=True, vmem_limit_bytes=budget
        ),
    )(
        tokens,
        coefs,
        w_gate,
        w_up,
        w_down,
        queries,
        k_cache.reshape(reqs, positions * kv_heads, head_dim),
        value_cache.reshape(reqs, positions * kv_heads, head_dim),
        lengths,
    )
    return routed, attn.reshape(reqs, -1)


def ring_local(budget, *args):
    tokens, gate_wts, expert_ids, replica, w_gate, w_up, w_down, queries, k_cache, value_cache, lengths = args
    devices = lax.axis_size("wide") * lax.axis_size("narrow")
    experts = 3 * devices // 2
    spares = devices // 2
    slot = jnp.where((replica == 1) & (expert_ids < spares), expert_ids + experts, expert_ids)
    lanes = -(-devices * SLOT_DEV // LANES) * LANES
    named = jnp.arange(lanes, dtype=jnp.int32)
    coefs = jnp.sum(
        jnp.where(slot[:, :, None] == named[None, None, :], gate_wts.astype(jnp.float32)[:, :, None], 0.0),
        axis=1,
    ).astype(jnp.bfloat16)
    return fused(tokens, coefs, w_gate, w_up, w_down, queries, k_cache, value_cache, lengths, budget)


def ring_bytes(count, tokens, w_gate, k_cache):
    rows, width = tokens.shape
    lanes = -(-count * 2 * SLOT_DEV // LANES) * LANES
    held = count * rows * (2 * (width + lanes) + 5 * width)
    weights = 3 * w_gate.size
    caches = 2 * k_cache.size
    return 2 * (held + weights + caches)


VMEM_BUDGET = 56 * 2**20
VMEM_HELD = 40 * 2**20


def local(*args):
    count, pair = lax.axis_size("wide"), lax.axis_size("narrow")
    kv_heads = args[8].shape[2]
    fits = ring_bytes(count, args[0], args[4], args[8]) <= VMEM_HELD
    shaped = (
        pair == 2
        and count >= 4
        and count % 2 == 0
        and args[0].shape[0] % 32 == 0
        and kv_heads & (kv_heads - 1) == 0
    )
    if fits and shaped:
        return ring_local(VMEM_BUDGET, *args)
    return exchange_local(*args)


def solution(mesh):
    in_specs = (
        P(("groups", "wide", "narrow"), None),
        P(("groups", "wide", "narrow"), None),
        P(("groups", "wide", "narrow"), None),
        P(("groups", "wide", "narrow"), None),
        P(("wide", "narrow"), None, None),
        P(("wide", "narrow"), None, None),
        P(("wide", "narrow"), None, None),
        P(("groups", "wide", "narrow"), None, None),
        P(("groups", "wide", "narrow"), None, None, None),
        P(("groups", "wide", "narrow"), None, None, None),
        P(("groups", "wide", "narrow")),
    )
    out_specs = (P(("groups", "wide", "narrow"), None), P(("groups", "wide", "narrow"), None))
    return jax.shard_map(local, mesh=mesh, in_specs=in_specs, out_specs=out_specs, check_vma=False)
```

```python
import functools
import jax
import jax.numpy as jnp
from jax import lax
from jax.experimental import pallas as pl
from jax.experimental.pallas import tpu as pltpu
from jax.sharding import PartitionSpec as P

SLOT_DEV = 2
LANES = 128
MESH = pl.DeviceIdType.MESH


def attend(queries, k_cache, value_cache, lengths):
    reqs, heads, head_dim = queries.shape
    kv_heads = k_cache.shape[2]
    group = heads // kv_heads
    grouped = queries.reshape(reqs, kv_heads, group, head_dim)
    scores = jnp.einsum(
        "rkgd,rlkd->rkgl", grouped, k_cache, preferred_element_type=jnp.float32
    ) * head_dim ** (-0.5)
    valid = jnp.arange(k_cache.shape[1], dtype=jnp.int32)[None, :] < lengths[:, None]
    valid = valid[:, None, None, :]
    scores = jnp.where(valid, scores, -1e30)
    top = jnp.max(scores, axis=-1, keepdims=True)
    expd = jnp.where(valid, jnp.exp(scores - top), 0.0)
    probs = (expd / jnp.sum(expd, axis=-1, keepdims=True)).astype(jnp.bfloat16)
    mixed = jnp.einsum("rkgl,rlkd->rkgd", probs, value_cache, preferred_element_type=jnp.float32)
    return mixed.astype(jnp.bfloat16).reshape(reqs, heads * head_dim)


def exchange_local(
    tokens,
    gate_wts,
    expert_ids,
    replica,
    w_gate,
    w_up,
    w_down,
    queries,
    k_cache,
    value_cache,
    lengths,
):
    wide_count = lax.axis_size("wide")
    narrow_count = lax.axis_size("narrow")
    devices = wide_count * narrow_count
    experts = 3 * devices // 2
    spares = devices // 2
    rows_here = tokens.shape[0]
    model_width = tokens.shape[1]
    top_count = expert_ids.shape[1]
    capacity = min(rows_here, 2 * rows_here * top_count // devices)
    phys_slot = jnp.where((replica == 1) & (expert_ids < spares), expert_ids + experts, expert_ids)
    owner_dev = phys_slot // SLOT_DEV
    slot_bit = phys_slot % SLOT_DEV
    owners = jnp.arange(devices, dtype=jnp.int32)
    hits_mask = owner_dev[:, :, None] == owners[None, None, :]
    routed_to = jnp.any(hits_mask, axis=1).astype(jnp.float32)
    gate_values = gate_wts.astype(jnp.float32)
    coefficients = jnp.stack(
        [
            jnp.sum(
                jnp.where(hits_mask & (slot_bit[:, :, None] == j), gate_values[:, :, None], 0.0),
                axis=1,
            )
            for j in range(SLOT_DEV)
        ],
        axis=-1,
    )
    row_ids = jnp.arange(rows_here, dtype=jnp.int32)
    earlier = (row_ids[None, :] < row_ids[:, None]).astype(jnp.float32)
    before = jnp.dot(earlier, routed_to, precision=lax.Precision.HIGHEST)
    positions = jnp.arange(capacity, dtype=jnp.float32)
    slots_map = (routed_to[:, :, None] * (before[:, :, None] == positions[None, None, :])).astype(
        jnp.bfloat16
    )
    outgoing = jnp.einsum(
        "rdc,rm->dcm", slots_map, tokens, preferred_element_type=jnp.float32
    ).astype(jnp.bfloat16)
    weights_out = jnp.einsum(
        "rdc,rdj->dcj",
        slots_map,
        coefficients.astype(jnp.bfloat16),
        preferred_element_type=jnp.float32,
    ).astype(jnp.bfloat16)
    arrived = lax.all_to_all(outgoing, ("wide", "narrow"), split_axis=0, concat_axis=0, tiled=True)
    shares = lax.all_to_all(
        weights_out, ("wide", "narrow"), split_axis=0, concat_axis=0, tiled=True
    )
    flat = arrived.reshape(-1, model_width)
    share_flat = shares.reshape(-1, SLOT_DEV).astype(jnp.float32)
    result = jnp.zeros(flat.shape, jnp.float32)
    for j in range(SLOT_DEV):
        gated = jnp.dot(flat, w_gate[j], preferred_element_type=jnp.float32)
        upward = jnp.dot(flat, w_up[j], preferred_element_type=jnp.float32)
        hidden = (jax.nn.silu(gated) * upward).astype(jnp.bfloat16)
        result = result + share_flat[:, j : j + 1] * jnp.dot(
            hidden, w_down[j], preferred_element_type=jnp.float32
        )
    returned = lax.all_to_all(
        result.astype(jnp.bfloat16).reshape(arrived.shape),
        ("wide", "narrow"),
        split_axis=0,
        concat_axis=0,
        tiled=True,
    )
    attn_out = attend(queries, k_cache, value_cache, lengths)
    routed_out = jnp.einsum(
        "rdc,dcm->rm", slots_map, returned, preferred_element_type=jnp.float32
    ).astype(jnp.bfloat16)
    return (routed_out, attn_out)


def ring_place(wide, count):
    odd = wide % 2
    return (1 - odd) * (wide // 2) + odd * (count - 1 - wide // 2)


def ring_wide(place, count):
    upper = place // (count // 2)
    return (1 - upper) * (2 * place) + upper * (2 * (count - 1 - place) + 1)


def kernel(
    count,
    kv_heads,
    lanes,
    x_ref,
    gate_wts_ref,
    ids_ref,
    replica_ref,
    gate_hbm,
    up_hbm,
    down_hbm,
    q_ref,
    k_hbm,
    v_hbm,
    len_ref,
    out_ref,
    attn_ref,
    xa,
    po,
    sb,
    rb,
    tb,
    w_in,
    w_out,
    k_buf,
    v_buf,
    w_sem,
    kv_sem,
    ag_send,
    ag_recv,
    sib_send,
    sib_recv,
    own_send,
    own_recv,
    part_send,
    part_recv,
    part0_send,
    part0_recv,
    rs_send,
    rs_recv,
):
    rows, width = x_ref.shape
    half = rows // 2
    hid = gate_hbm.shape[2]
    arrivals = count - 1
    wide = lax.axis_index("wide")
    core = lax.axis_index("narrow")
    other = 1 - core
    place = ring_place(wide, count)
    after = ring_wide((place + 1) % count, count)
    before = ring_wide((place + count - 1) % count, count)
    me = wide * 2 + core
    targets = ({"wide": after}, {"wide": before})
    sibling = {"narrow": other}

    def aligned(index, size):
        return pl.ds(pl.multiple_of(index * size, size), size)

    def remote(src, dst, send, recv, device):
        return pltpu.make_async_remote_copy(
            src_ref=src, dst_ref=dst, send_sem=send, recv_sem=recv, device_id=device, device_id_type=MESH
        )

    kv_copies = [
        pltpu.make_async_copy(k_hbm, k_buf, kv_sem.at[0]),
        pltpu.make_async_copy(v_hbm, v_buf, kv_sem.at[1]),
    ]
    w_copies = []
    for j in range(SLOT_DEV):
        w_copies += [
            pltpu.make_async_copy(
                gate_hbm.at[j], w_in.at[:, pl.ds(2 * j * hid, hid)], w_sem.at[3 * j]
            ),
            pltpu.make_async_copy(
                up_hbm.at[j], w_in.at[:, pl.ds((2 * j + 1) * hid, hid)], w_sem.at[3 * j + 1]
            ),
            pltpu.make_async_copy(
                down_hbm.at[j], w_out.at[pl.ds(j * hid, hid)], w_sem.at[3 * j + 2]
            ),
        ]
    for copy in kv_copies + w_copies:
        copy.start()
    barrier = pltpu.get_barrier_semaphore()
    for device in (*targets, sibling):
        pl.semaphore_signal(barrier, inc=1, device_id=device, device_id_type=MESH)
    xa[0, aligned(core, rows), :width] = x_ref[...]
    ids = ids_ref[...]
    moved = (replica_ref[...] == 1) & (ids < count)
    slot = jnp.where(moved, ids + 3 * count, ids)
    gate_values = gate_wts_ref[...].astype(jnp.float32)
    named = lax.broadcasted_iota(jnp.int32, (lanes, rows), 0)
    coefs = jnp.zeros((lanes, rows), jnp.float32)
    for k in range(ids.shape[0]):
        coefs = coefs + jnp.where(named == slot[k : k + 1], gate_values[k : k + 1], 0.0)
    xa[0, aligned(core, rows), width:] = coefs.T.astype(jnp.bfloat16)

    pl.semaphore_wait(barrier, 3)

    def unit(i, way):
        return i + 1, aligned(way * 2 + core, half)

    def gather_own(i, way):
        piece, at = unit(i, way)
        part = i if way == 0 else 1 - i
        return remote(
            xa.at[0, aligned(core * 2 + part, half)],
            xa.at[piece, at],
            ag_send.at[way, i],
            ag_recv.at[way, i],
            targets[way],
        )

    def gather_on(i, way):
        piece, at = unit(i, way)
        return remote(
            xa.at[piece - 2, at], xa.at[piece, at], ag_send.at[way, i], ag_recv.at[way, i], targets[way]
        )

    def landed(i, way):
        piece, at = unit(i, way)
        return remote(
            xa.at[piece, at], xa.at[piece, at], ag_send.at[way, i], ag_recv.at[way, i], targets[way]
        )

    def share(i, way):
        piece, at = unit(i, way)
        return remote(xa.at[piece, at], xa.at[piece, at], sib_send.at[way, i], sib_recv.at[way, i], sibling)

    def share_own():
        at = aligned(core, rows)
        return remote(xa.at[0, at], xa.at[0, at], own_send, own_recv, sibling)

    def give(i, way):
        return remote(
            po.at[i + 1, aligned(way * 2 + other, half)],
            sb.at[i + 1, pl.ds(way * half, half)],
            part_send.at[way, i],
            part_recv.at[way, i],
            sibling,
        )

    def give_own():
        return remote(po.at[0, aligned(other, rows)], sb.at[0], part0_send, part0_recv, sibling)

    def collect(r, way):
        return remote(tb.at[way, r], rb.at[way, r], rs_send.at[way, r], rs_recv.at[way, r], targets[1 - way])

    for i in range(2):
        for way in range(2):
            gather_own(i, way).start()
    share_own().start()

    for copy in kv_copies:
        copy.wait()
    heads, head_dim = q_ref.shape[1:]
    group = heads // kv_heads
    shape = (heads, k_buf.shape[1])
    col = lax.broadcasted_iota(jnp.int32, shape, 1)
    row = lax.broadcasted_iota(jnp.int32, shape, 0)
    kind = jnp.zeros(shape, jnp.int32)
    for g in range(1, kv_heads):
        kind = kind + (row >= g * group).astype(jnp.int32)
    mine = jnp.bitwise_and(col, kv_heads - 1) == kind
    flat = []
    for r in range(q_ref.shape[0]):
        scores = lax.dot_general(
            q_ref[r], k_buf[r], (((1,), (1,)), ((), ())), preferred_element_type=jnp.float32
        ) * head_dim ** (-0.5)
        valid = mine & (col < len_ref[r] * kv_heads)
        scores = jnp.where(valid, scores, -1e30)
        top = jnp.max(scores, axis=-1, keepdims=True)
        expd = jnp.where(valid, jnp.exp(scores - top), 0.0)
        probs = (expd / jnp.sum(expd, axis=-1, keepdims=True)).astype(jnp.bfloat16)
        mixed = jnp.dot(probs, v_buf[r], preferred_element_type=jnp.float32)
        flat.append(jnp.concatenate([mixed[h : h + 1] for h in range(heads)], axis=1))
    attn_ref[...] = jnp.concatenate(flat, axis=0).astype(jnp.bfloat16)

    def experts(t):
        x = xa[t, :, :width]
        shares = xa[t, :, width:].astype(jnp.float32)
        lane = lax.broadcasted_iota(jnp.int32, shares.shape, 1)
        hidden = []
        for j in range(SLOT_DEV):
            both = jnp.dot(
                x, w_in[:, 2 * j * hid : 2 * (j + 1) * hid], preferred_element_type=jnp.float32
            )
            gated, upward = both[:, :hid], both[:, hid:]
            weight = jnp.sum(
                jnp.where(lane == me * SLOT_DEV + j, shares, 0.0), axis=1, keepdims=True
            )
            hidden.append((weight * (gated / (1.0 + jnp.exp(-gated)) * upward)).astype(jnp.bfloat16))
        hidden = jnp.concatenate(hidden, axis=1)
        po[t] = jnp.dot(hidden, w_out[...], preferred_element_type=jnp.float32).astype(jnp.bfloat16)

    def back(r, first):
        i = arrivals - 1 - r
        for way in range(2):
            give(i, way).wait_recv()
            piece, at = unit(i, way)
            total = po[piece, at].astype(jnp.float32) + sb[piece, way * half : (way + 1) * half].astype(
                jnp.float32
            )
            if not first:
                collect(r - 2, way).wait_recv()
                total = total + rb[way, r - 2].astype(jnp.float32)
            tb[way, r] = total.astype(jnp.bfloat16)
            collect(r, way).start()

    def step(t, _):
        @pl.when(t == 0)
        def _():
            share_own().wait_recv()
            for copy in w_copies:
                copy.wait()

        @pl.when(t > 0)
        def _():
            for way in range(2):
                share(t - 1, way).wait_recv()

        experts(t)

        @pl.when(t == 0)
        def _():
            give_own().start()

        @pl.when(t > 0)
        def _():
            for way in range(2):
                give(t - 1, way).start()

        @pl.when(t < arrivals)
        def _():
            for way in range(2):
                landed(t, way).wait_recv()

            @pl.when(t + 2 < arrivals)
            def _():
                for way in range(2):
                    gather_on(t + 2, way).start()

            for way in range(2):
                share(t, way).start()

        @pl.when(t == arrivals - 1)
        def _():
            back(1, True)

        return _

    lax.fori_loop(0, count, step, None)
    back(0, True)

    def back_on(r, _):
        back(r, False)
        return _

    lax.fori_loop(2, arrivals, back_on, None)

    give_own().wait_recv()
    for way in range(2):
        collect(arrivals - 2, way).wait_recv()
        collect(arrivals - 1, way).wait_recv()
    for part in range(2):
        total = po[0, aligned(core * 2 + part, half)].astype(jnp.float32) + sb[
            0, part * half : (part + 1) * half
        ].astype(jnp.float32)
        for way in range(2):
            i = part if way == 0 else 1 - part
            total = total + rb[way, arrivals - 1 - i].astype(jnp.float32)
        out_ref[part * half : (part + 1) * half] = total.astype(jnp.bfloat16)

    share_own().wait_send()
    give_own().wait_send()

    def drain(i, _):
        for way in range(2):
            landed(i, way).wait_send()
            share(i, way).wait_send()
            give(i, way).wait_send()
            collect(i, way).wait_send()
        return _

    lax.fori_loop(0, arrivals, drain, None)


def fused(tokens, gate_wts, expert_ids, replica, w_gate, w_up, w_down, queries, k_cache, value_cache, lengths, budget):
    count = lax.axis_size("wide")
    rows, width = tokens.shape
    half = rows // 2
    lanes = -(-count * 2 * SLOT_DEV // LANES) * LANES
    hid = w_gate.shape[2]
    reqs, positions, kv_heads, head_dim = k_cache.shape
    bf16, dma = jnp.bfloat16, pltpu.SemaphoreType.DMA
    vmem, hbm = pl.BlockSpec(memory_space=pltpu.VMEM), pl.BlockSpec(memory_space=pl.ANY)
    arrivals = count - 1
    pairs = dma((2, arrivals))
    routed, attn = pl.pallas_call(
        functools.partial(kernel, count, kv_heads, lanes),
        out_shape=(
            jax.ShapeDtypeStruct(tokens.shape, bf16),
            jax.ShapeDtypeStruct((reqs, queries.shape[1] * head_dim), bf16),
        ),
        in_specs=[vmem, vmem, vmem, vmem, hbm, hbm, hbm, vmem, hbm, hbm, pl.BlockSpec(memory_space=pltpu.SMEM)],
        out_specs=(vmem, vmem),
        scratch_shapes=[
            pltpu.VMEM((count, 2 * rows, width + lanes), bf16),
            pltpu.VMEM((count, 2 * rows, width), bf16),
            pltpu.VMEM((count, rows, width), bf16),
            pltpu.VMEM((2, arrivals, half, width), bf16),
            pltpu.VMEM((2, arrivals, half, width), bf16),
            pltpu.VMEM((width, 2 * SLOT_DEV * hid), bf16),
            pltpu.VMEM((SLOT_DEV * hid, width), bf16),
            pltpu.VMEM((reqs, positions * kv_heads, head_dim), bf16),
            pltpu.VMEM((reqs, positions * kv_heads, head_dim), bf16),
            dma((3 * SLOT_DEV,)),
            dma((2,)),
            pairs,
            pairs,
            pairs,
            pairs,
            dma(()),
            dma(()),
            pairs,
            pairs,
            dma(()),
            dma(()),
            pairs,
            pairs,
        ],
        compiler_params=pltpu.CompilerParams(
            collective_id=0, has_side_effects=True, vmem_limit_bytes=budget
        ),
    )(
        tokens,
        gate_wts.T,
        expert_ids.T,
        replica.T,
        w_gate,
        w_up,
        w_down,
        queries,
        k_cache.reshape(reqs, positions * kv_heads, head_dim),
        value_cache.reshape(reqs, positions * kv_heads, head_dim),
        lengths,
    )
    return routed, attn


def ring_bytes(count, tokens, w_gate, k_cache):
    rows, width = tokens.shape
    lanes = -(-count * 2 * SLOT_DEV // LANES) * LANES
    held = count * rows * (2 * (width + lanes) + 5 * width)
    weights = 3 * w_gate.size
    caches = 2 * k_cache.size
    return 2 * (held + weights + caches)


VMEM_BUDGET = 56 * 2**20
VMEM_HELD = 40 * 2**20


def local(*args):
    count, pair = lax.axis_size("wide"), lax.axis_size("narrow")
    kv_heads = args[8].shape[2]
    fits = ring_bytes(count, args[0], args[4], args[8]) <= VMEM_HELD
    shaped = (
        pair == 2
        and count >= 4
        and count % 2 == 0
        and args[0].shape[0] % 32 == 0
        and kv_heads & (kv_heads - 1) == 0
    )
    if fits and shaped:
        return fused(*args, VMEM_BUDGET)
    return exchange_local(*args)


def solution(mesh):
    in_specs = (
        P(("groups", "wide", "narrow"), None),
        P(("groups", "wide", "narrow"), None),
        P(("groups", "wide", "narrow"), None),
        P(("groups", "wide", "narrow"), None),
        P(("wide", "narrow"), None, None),
        P(("wide", "narrow"), None, None),
        P(("wide", "narrow"), None, None),
        P(("groups", "wide", "narrow"), None, None),
        P(("groups", "wide", "narrow"), None, None, None),
        P(("groups", "wide", "narrow"), None, None, None),
        P(("groups", "wide", "narrow")),
    )
    out_specs = (P(("groups", "wide", "narrow"), None), P(("groups", "wide", "narrow"), None))
    return jax.shard_map(local, mesh=mesh, in_specs=in_specs, out_specs=out_specs, check_vma=False)
```
